256 devices in a mesh: dp: 16 (over y, z_lo), owner: 16 (over x, z_hi, core).
Axes of the slice: x: 4, y: 4, z: 8 (z_hi: 2, z_lo: 4; z = z_hi * 4 + z_lo), core: 2. Of those that a mesh axis runs over, the one named last changes fastest.
Arguments:
- inputs: bfloat16 [8192, 4096], P('dp'), may hold values from -6 to 6
- out_grads: bfloat16 [8192, 16384], P('dp', 'owner'), may hold values from -0.0625 to 0.0625
- basis_in: bfloat16 [1024, 4096], P(None, 'owner'), may hold values from -0.1875 to 0.1875
- basis_out: bfloat16 [1024, 16384], P(None, 'owner'), may hold values from -0.1875 to 0.1875
- eigenvalues: float32 [4096, 16384], P('dp', 'owner'), may hold values from 0.2 to 5
Outputs:
- precond: bfloat16 [4096, 16384], P('dp', 'owner')
The draws below stay inside these ranges and needn't reach their ends.
All inputs are finite; a program needn't handle non-finite values.
Results may differ from the reference program's by a relative error of at most 0.023.
Values may be sent and summed in bfloat16 or wider, within the bound.
No kernel may reach another device: no remote copies, remote signals or barrier semaphores. Data moves between devices by JAX's collectives and lax.ppermute only.
A program may use at most 64 MiB of HBM per device.

```python
import math
import jax
import jax.numpy as jnp
from jax import lax

DA = 4096
FS = 16384
BLK = 1024
TOK_DEV = 512
TOKENS = 8192
N_DP = 16


def shard_levels(own_key, dims, shards, low, high):
    def one(dim, parts):
        draws = jax.random.uniform(jax.random.fold_in(jax.random.fold_in(own_key, 6), dim), (parts,), jnp.float32, low / len(shards), high / len(shards))
        return jnp.repeat(jnp.exp(draws), dims[dim] // parts).reshape((-1,) + (1,) * (len(dims) - dim - 1))

    gain = one(*shards[0])
    for cut in shards[1:]:
        gain = gain * one(*cut)
    return gain


def noise(own_key, extent, deviation, reach, split=(), held_as=jnp.bfloat16):
    array = deviation * jax.random.normal(own_key, extent, jnp.float32)
    if split:
        array = array * shard_levels(own_key, extent, split, -0.22, 0.18)
    return jnp.clip(array, -reach, reach).astype(held_as)


def setup_inputs(seed: int = 0) -> dict:
    key_list = jax.random.split(jax.random.key(seed), 6)
    return {
        "inputs": noise(key_list[0], (TOKENS, DA), 1.0, 6.0, ((0, 16),)),
        "out_grads": noise(key_list[1], (TOKENS, FS), TOKENS ** -0.5, 0.0625, ((0, 16), (1, 16))),
        "basis_in": noise(key_list[2], (BLK, DA), BLK ** -0.5, 0.1875, ((1, 16),)),
        "basis_out": noise(key_list[3], (BLK, FS), BLK ** -0.5, 0.1875, ((1, 16),)),
        "eigenvalues": jnp.clip(jnp.exp(math.log(5.0) - 3.218876 * jax.random.uniform(key_list[4], (DA, FS), jnp.float32) ** shard_levels(key_list[4], (DA, FS), ((0, 16), (1, 16)), -0.2, 0.2)), 0.2, 5.0),
    }


DAMPING = 0.05


def reference(inputs, out_grads, basis_in, basis_out, eigenvalues):
    in_blocks = DA // BLK
    out_blocks = FS // BLK
    input_basis = basis_in.astype(jnp.float32).reshape(BLK, in_blocks, BLK)
    output_basis = basis_out.astype(jnp.float32).reshape(BLK, out_blocks, BLK)
    input_rot = jnp.einsum("tbr,rbk->tbk", inputs.astype(jnp.float32).reshape(TOKENS, in_blocks, BLK), input_basis)
    input_rot = input_rot.reshape(TOKENS, DA).astype(jnp.bfloat16)
    grad_rot = jnp.einsum("tsj,jsl->tsl", out_grads.astype(jnp.float32).reshape(TOKENS, out_blocks, BLK), output_basis)
    grad_rot = grad_rot.reshape(TOKENS, FS).astype(jnp.bfloat16)
    input_parts = input_rot.reshape(N_DP, TOK_DEV, DA)
    grad_parts = grad_rot.reshape(N_DP, TOK_DEV, FS)

    def add_part(total, shard_pair):
        rotated_x, rotated_g = shard_pair
        partial_value = jnp.dot(rotated_x.T, rotated_g, preferred_element_type=jnp.float32)
        partial_value = lax.optimization_barrier(partial_value.astype(jnp.bfloat16))
        return total + partial_value.astype(jnp.float32), None

    projected, _ = lax.scan(add_part, jnp.zeros((DA, FS), jnp.float32), (input_parts, grad_parts))
    scaled = (projected / (eigenvalues + DAMPING)).astype(jnp.bfloat16)
    rotated_right = jnp.einsum("knl,jnl->knj", scaled.astype(jnp.float32).reshape(DA, out_blocks, BLK), output_basis)
    rotated_right = rotated_right.reshape(DA, FS).astype(jnp.bfloat16)
    precond = jnp.einsum("ibk,bkj->bij", input_basis, rotated_right.astype(jnp.float32).reshape(in_blocks, BLK, FS))
    return precond.reshape(DA, FS).astype(jnp.bfloat16)
```

```python
import jax
import jax.numpy as jnp
from jax import lax
from jax.sharding import PartitionSpec as P

DAMPING = 0.05
NX, NY, NZ = 4, 4, 4
L_PARTS = 1
K_PARTS = 1
BF = jnp.bfloat16
F32 = jnp.float32


def moved(block, place):
    route = []
    for y in range(NY):
        for z in range(NZ):
            for x in range(NX):
                for h in range(2):
                    for c in range(2):
                        to = place(x, y, z, h, c)
                        if to is None:
                            continue
                        tx, ty, tz, th, tc = to
                        source = (y * NZ + z) * 16 + x * 4 + h * 2 + c
                        target = (ty % NY * NZ + tz) * 16 + tx % NX * 4 + th * 2 + tc
                        route.append((source, target))
    return lax.ppermute(block, ("dp", "owner"), route)


def along_x(block, k):
    return moved(block, lambda x, y, z, h, c: (x + k, y, z, h, c))


def along_y(block, k):
    return moved(block, lambda x, y, z, h, c: (x, y + k, z, h, c))


def z_step(block, k, sources):
    return moved(block, lambda x, y, z, h, c: (x, y, z + k, h, c) if z in sources else None)


def from_diagonal(block, k):
    return moved(block, lambda x, y, z, h, c: (x + k, y, z, h, c) if x == y else None)


def other_half(block):
    return moved(block, lambda x, y, z, h, c: (x, y, z, 1 - h, c))


def other_core(block):
    return moved(block, lambda x, y, z, h, c: (x, y, z, h, 1 - c))


def dot(a, b, dims):
    return lax.dot_general(a, b, ((dims[:1], dims[1:]), ((), ())), preferred_element_type=F32)


def on_device(inputs, out_grads, basis_in, basis_out, eigenvalues):
    tok = inputs.shape[0]
    block = basis_in.shape[0]
    quarter = block // 4
    half = tok // 2
    owner = lax.axis_index("owner")
    data = lax.axis_index("dp")
    x, h, c = owner // 4, owner // 2 % 2, owner % 2
    y, z = data // NZ, data % NZ
    hc = owner % 4

    def basis_piece(k):
        return lax.dynamic_slice_in_dim(basis_in, (x + k) % NX * quarter, quarter, 0)

    piece = jnp.where(x == y, basis_piece(0), jnp.zeros((), BF))
    for k in (1, 3, 2):
        piece = piece + from_diagonal(basis_piece(k), k)
    pieces = jnp.stack([piece, other_half(piece)])
    mine = [pieces] + [along_x(pieces, k) for k in (1, 2, 3)]
    mine = jnp.stack(mine, 1)
    both = jnp.stack([mine, other_core(mine)], 1).reshape(4, block, quarter)

    own_half = lax.dynamic_slice_in_dim(inputs, c * half, half, 0)
    rest_half = lax.dynamic_slice_in_dim(inputs, (1 - c) * half, half, 0)

    def columns(rows, b, at):
        return lax.dynamic_slice_in_dim(rows, b % NY * block + at % NX * quarter, quarter, 1)

    got = jnp.stack([along_y(columns(own_half, y + k, x), k) for k in (1, 2, 3)])
    got = jnp.stack([got] + [along_x(got, k) for k in (1, 2, 3)])
    got_other = other_core(got)
    x_all = []
    for j in range(NX):
        x_all.append(
            jnp.concatenate(
                [columns(own_half, y, x - j), columns(rest_half, y, x - j)]
                + [got[j].reshape(3 * half, quarter), got_other[j].reshape(3 * half, quarter)],
                0,
            )
        )
    x_all = jnp.concatenate(x_all, 1)

    og_own = lax.dynamic_slice_in_dim(out_grads, c * half, half, 0)
    og_rest = lax.dynamic_slice_in_dim(out_grads, (1 - c) * half, half, 0)
    lw = block // L_PARTS
    kw = quarter // K_PARTS
    m_parts = []
    for g in range(L_PARTS):
        s_part = basis_out[:, g * lw : (g + 1) * lw]
        gt = jnp.stack([dot(s_part, og_own, (0, 1)), dot(s_part, og_rest, (0, 1))]).astype(BF)
        others = [along_y(gt, k) for k in (1, 2, 3)]
        g_all = jnp.concatenate(
            [gt[0], gt[1]] + [o[0] for o in others] + [o[1] for o in others], 1
        )
        m_parts.append(dot(g_all, x_all, (1, 0)).astype(BF))

    inverse = (1.0 / (eigenvalues + DAMPING)).T

    def basis_for(d):
        return lax.dynamic_index_in_dim(both, (z + d) % NZ ^ hc, 0, keepdims=False)

    bases = [basis_for(d) for d in range(4)]
    row_at = (x - z) % NX * quarter
    rows = [lax.dynamic_slice_in_dim(b, row_at, quarter, 0) for b in bases]
    out = None
    for n in range(K_PARTS):
        cols = slice(n * kw, (n + 1) * kw)
        scaled = []
        for g in range(L_PARTS):
            part = [dot(m_parts[g], bases[d][:, cols], (1, 0)) for d in range(4)]
            low = z == 0
            first = jnp.where(low, part[3], part[1]).astype(BF)
            up = z_step(first, 1, (0,))
            down = z_step(first, -1, (3,))
            up = z_step((part[2] + up.astype(F32)).astype(BF), 1, (0, 1))
            down = z_step((part[2] + down.astype(F32)).astype(BF), -1, (2, 3))
            up = z_step((part[1] + up.astype(F32)).astype(BF), 1, (0, 1, 2))
            down = z_step((part[3] + down.astype(F32)).astype(BF), -1, (1, 2, 3))
            total = part[0] + up.astype(F32) + down.astype(F32)
            scaled.append((total * inverse[g * lw : (g + 1) * lw, cols]).astype(BF))
        right = dot(basis_out, jnp.concatenate(scaled, 0), (1, 0)).astype(BF)
        up1 = z_step(right, 1, (0, 1, 2))
        down1 = z_step(right, -1, (1, 2, 3))
        up2 = z_step(up1, 1, (1, 2))
        down2 = z_step(down1, -1, (1, 2))
        up3 = z_step(up2, 1, (2,))
        down3 = z_step(down2, -1, (1,))
        for d, r in enumerate((right, down1 + up3, down2 + up2, up1 + down3)):
            term = dot(rows[d][:, cols], r, (1, 1))
            out = term if out is None else out + term
    return out.astype(BF)


def solution(mesh):
    placed = (P("dp", None), P("dp", "owner"), P(None, "owner"), P(None, "owner"), P("dp", "owner"))
    return jax.shard_map(
        on_device, mesh=mesh, in_specs=placed, out_specs=P("dp", "owner"), check_vma=False
    )
```

```python
import functools

import jax
import jax.numpy as jnp
from jax import lax
from jax.experimental import pallas as pl
from jax.experimental.pallas import tpu as pltpu
from jax.sharding import PartitionSpec as P

DAMPING = 0.05
NX, NY, NZ = 4, 4, 4
L_PARTS = 2
BF = jnp.bfloat16
F32 = jnp.float32


def moved(block, place):
    route = []
    for y in range(NY):
        for z in range(NZ):
            for x in range(NX):
                for h in range(2):
                    for c in range(2):
                        to = place(x, y, z, h, c)
                        if to is None:
                            continue
                        tx, ty, tz, th, tc = to
                        source = (y * NZ + z) * 16 + x * 4 + h * 2 + c
                        target = (ty % NY * NZ + tz) * 16 + tx % NX * 4 + th * 2 + tc
                        route.append((source, target))
    return lax.ppermute(block, ("dp", "owner"), route)


def along_x(block, k):
    return moved(block, lambda x, y, z, h, c: (x + k, y, z, h, c))


def along_y(block, k):
    return moved(block, lambda x, y, z, h, c: (x, y + k, z, h, c))


def z_step(block, steps):
    return moved(block, lambda x, y, z, h, c: (x, y, z + steps[z], h, c) if z in steps else None)


def crossed(block, flip):
    return moved(block, lambda x, y, z, h, c: (y, x, z, h ^ flip, c))


def other_core(block):
    return moved(block, lambda x, y, z, h, c: (x, y, z, h, 1 - c))


def dot(a, b, dims):
    return lax.dot_general(a, b, ((dims[:1], dims[1:]), ((), ())), preferred_element_type=F32)


def product_kernel(place, g0, g1, g2, g3, local, *rest):
    own, other, out, held = rest[0:4], rest[4:8], rest[8], rest[9]
    z, h, c = place[0], place[1], place[2]
    grads = (g0, g1, g2, g3)
    half = local.shape[2]
    quarter = local.shape[3]
    rows = out.shape[1]
    tile = min(256, rows)

    for j in range(4):
        for r in range(rows // tile):
            at = slice(r * tile, (r + 1) * tile)
            acc = dot(g0[at, 0:half], local[0, j], (1, 0))
            acc += dot(g0[at, half : 2 * half], local[1, j], (1, 0))
            for k in range(1, 4):
                acc += dot(grads[k][at, 0:half], own[j][k - 1], (1, 0))
                acc += dot(grads[k][at, half : 2 * half], other[j][k - 1], (1, 0))
            held[at, j * quarter : (j + 1) * quarter] = acc.astype(BF)
    for d in range(4):
        q = lax.rem(z + d, 4)
        hrel = jnp.bitwise_xor(lax.shift_right_logical(q, 1), h)
        crel = jnp.bitwise_xor(jnp.bitwise_and(q, 1), c)
        for r in range(rows // tile):
            at = slice(r * tile, (r + 1) * tile)
            acc = None
            for j in range(4):
                basis = jnp.where(crel == 0, own[j][3 + hrel], other[j][3 + hrel])
                term = dot(held[at, j * quarter : (j + 1) * quarter], basis, (1, 0))
                acc = term if acc is None else acc + term
            out[d, at, :] = acc.astype(BF)


def product(place, grads, local, own, other):
    rows = grads[0].shape[0]
    quarter = local.shape[3]
    flops = 2 * rows * 4 * quarter * (2 * 4 * local.shape[2] + 4 * quarter)
    return pl.pallas_call(
        product_kernel,
        out_shape=jax.ShapeDtypeStruct((4, rows, quarter), BF),
        in_specs=[pl.BlockSpec(memory_space=pltpu.SMEM)] + [pl.BlockSpec(memory_space=pltpu.VMEM)] * 13,
        out_specs=pl.BlockSpec(memory_space=pltpu.VMEM),
        scratch_shapes=[pltpu.VMEM((rows, 4 * quarter), BF)],
        compiler_params=pltpu.CompilerParams(vmem_limit_bytes=40 << 20),
        cost_estimate=pl.CostEstimate(flops=flops, bytes_accessed=12 << 20, transcendentals=0),
    )(place, *grads, local, *own, *other)


def back_kernel(place, basis, s, u1, d1, u2, d2, r3, out):
    z = place[0]
    far = jnp.where(z == 3, basis[1], basis[3])
    acc = dot(basis[0], s[...], (1, 1))
    acc += dot(basis[3], u1[...], (1, 1))
    acc += dot(basis[1], d1[...], (1, 1))
    acc += dot(basis[2], u2[...] + d2[...], (1, 1))
    acc += dot(far, r3[...], (1, 1))
    out[...] = acc.astype(BF)


def back(place, basis, parts):
    rows, quarter = parts[0].shape
    return pl.pallas_call(
        back_kernel,
        out_shape=jax.ShapeDtypeStruct((quarter, rows), BF),
        in_specs=[pl.BlockSpec(memory_space=pltpu.SMEM)] + [pl.BlockSpec(memory_space=pltpu.VMEM)] * 7,
        out_specs=pl.BlockSpec(memory_space=pltpu.VMEM),
        compiler_params=pltpu.CompilerParams(vmem_limit_bytes=24 << 20),
        cost_estimate=pl.CostEstimate(
            flops=10 * rows * quarter * quarter, bytes_accessed=2 << 20, transcendentals=0
        ),
    )(place, basis, *parts)


def on_device(inputs, out_grads, basis_in, basis_out, eigenvalues):
    tok = inputs.shape[0]
    block = basis_in.shape[0]
    quarter = block // 4
    half = tok // 2
    owner = lax.axis_index("owner")
    data = lax.axis_index("dp")
    x, h, c = owner // 4, owner // 2 % 2, owner % 2
    y, z = data // NZ, data % NZ
    place = jnp.stack([z, h, c, x]).astype(jnp.int32)
    lw = block // L_PARTS

    piece = lax.dynamic_slice_in_dim(basis_in, y * quarter, quarter, 0)
    pieces = jnp.stack([crossed(piece, 0), crossed(piece, 1)])

    og = jnp.concatenate(
        [
            lax.dynamic_slice_in_dim(out_grads, c * half, half, 0),
            lax.dynamic_slice_in_dim(out_grads, (1 - c) * half, half, 0),
        ],
        0,
    )
    gts = [
        dot(basis_out[:, g * lw : (g + 1) * lw], og, (0, 1)).astype(BF) for g in range(L_PARTS)
    ]
    gts[0], inputs = lax.optimization_barrier((gts[0], inputs))

    own_half = lax.dynamic_slice_in_dim(inputs, c * half, half, 0)
    rest_half = lax.dynamic_slice_in_dim(inputs, (1 - c) * half, half, 0)

    def columns(rows, b, at):
        return lax.dynamic_slice_in_dim(rows, b % NY * block + at % NX * quarter, quarter, 1)

    got = jnp.stack([along_y(columns(own_half, y + k, x), k) for k in (1, 2, 3)])
    got = jnp.concatenate([got, pieces], 0)
    own = [got] + [along_x(got, k) for k in (1, 2, 3)]
    other = [other_core(o) for o in own]
    local = jnp.stack(
        [jnp.stack([columns(rows, y, x - j) for j in range(NX)]) for rows in (own_half, rest_half)]
    )

    inverse = (1.0 / (eigenvalues + DAMPING)).T

    row_at = (x - z) % NX

    def basis_rows(d):
        q = (z + d) % NZ
        hrel, crel = q // 2 ^ h, q % 2 ^ c
        all_j = jnp.stack(own + other)
        return lax.dynamic_slice(
            all_j, (crel * 4 + row_at, 3 + hrel, 0, 0), (1, 1, quarter, quarter)
        ).reshape(quarter, quarter)

    rows = jnp.stack([basis_rows(d) for d in range(4)])

    out = None
    for g in range(L_PARTS):
        gt = gts[g]
        grads = [gt] + [along_y(gt, k) for k in (1, 2, 3)]
        part = product(place, grads, local, own, other)
        first = lax.dynamic_index_in_dim(part, jnp.where(z == 0, 3, 1), 0, keepdims=False)
        r1 = z_step(first, {0: 1, 3: -1})
        t2 = (part[2].astype(F32) + r1.astype(F32)).astype(BF)
        u2 = z_step(t2, {0: 1, 1: 1})
        d2 = z_step(t2, {3: -1, 2: -1})
        u3 = z_step((part[1].astype(F32) + u2.astype(F32)).astype(BF), {0: 1, 1: 1, 2: 1})
        d3 = z_step((part[3].astype(F32) + d2.astype(F32)).astype(BF), {3: -1, 2: -1, 1: -1})
        total = part[0].astype(F32) + u3.astype(F32) + d3.astype(F32)
        s = (total * inverse[g * lw : (g + 1) * lw]).astype(BF)
        u1 = z_step(s, {0: 1, 1: 1, 2: 1})
        d1 = z_step(s, {3: -1, 2: -1, 1: -1})
        u2 = z_step(u1, {1: 1, 2: 1})
        d2 = z_step(d1, {2: -1, 1: -1})
        r3 = z_step(u2 + d2, {2: 1, 1: -1})
        b = back(place, rows, (s, u1, d1, u2, d2, r3))
        term = dot(b, basis_out[:, g * lw : (g + 1) * lw], (1, 1))
        out = term if out is None else out + term
    return out.astype(BF)


def solution(mesh):
    placed = (P("dp", None), P("dp", "owner"), P(None, "owner"), P(None, "owner"), P("dp", "owner"))
    return jax.shard_map(
        on_device, mesh=mesh, in_specs=placed, out_specs=P("dp", "owner"), check_vma=False
    )
```

```python
import functools

import jax
import jax.numpy as jnp
from jax import lax
from jax.experimental import pallas as pl
from jax.experimental.pallas import tpu as pltpu
from jax.sharding import PartitionSpec as P

DAMPING = 0.05
NX, NY, NZ = 4, 4, 4
BF = jnp.bfloat16
F32 = jnp.float32


def moved(block, place):
    route = []
    for y in range(NY):
        for z in range(NZ):
            for x in range(NX):
                for h in range(2):
                    for c in range(2):
                        tx, ty, tz, th, tc = place(x, y, z, h, c)
                        source = (y * NZ + z) * 16 + x * 4 + h * 2 + c
                        target = (ty % NY * NZ + tz % NZ) * 16 + tx % NX * 4 + th * 2 + tc
                        route.append((source, target))
    return lax.ppermute(block, ("dp", "owner"), route)


def along_x(block, k):
    return moved(block, lambda x, y, z, h, c: (x + k, y, z, h, c))


def along_y(block, k):
    return moved(block, lambda x, y, z, h, c: (x, y + k, z, h, c))


def across_z(block, e):
    return moved(block, lambda x, y, z, h, c: (x, y, z ^ e, h, c))


def crossed(block, flip):
    return moved(block, lambda x, y, z, h, c: (y, x, z, h ^ flip, c))


def other_core(block):
    return moved(block, lambda x, y, z, h, c: (x, y, z, h, 1 - c))


def dot(a, b, dims):
    return lax.dot_general(a, b, ((dims[:1], dims[1:]), ((), ())), preferred_element_type=F32)


def vmem(count):
    return [pl.BlockSpec(memory_space=pltpu.VMEM)] * count


def scalars():
    return [pl.BlockSpec(memory_space=pltpu.SMEM)]


def product_kernel(start, place, g0, g1, g2, g3, mine, rest, *refs):
    count = len(refs) - 12
    own, other, outs = refs[0:4], refs[4:8], refs[8 : 8 + count]
    g_held, m_held, x_held, sems = refs[8 + count :]
    x = place[3]
    half = mine.shape[0]
    rows = outs[0].shape[0]
    total = count * rows
    copies = []

    def fetch(source, target):
        copies.append(pltpu.make_async_copy(source, target, sems.at[len(copies)]))
        copies[-1].start()

    fetch(g0.at[pl.ds(start, total)], g_held.at[0])
    fetch(mine, m_held.at[0])
    fetch(rest, m_held.at[1])
    for k, g in enumerate((g1, g2, g3)):
        fetch(g.at[pl.ds(start, total)], g_held.at[k + 1])
    first = len(copies)
    for j in range(4):
        fetch(own[j], x_held.at[0, j])
        fetch(other[j], x_held.at[1, j])
    for copy in copies[:first]:
        copy.wait()
    for j in range(4):
        cols = pl.ds(pl.multiple_of(lax.rem(x + 4 - j, 4) * half, half), half)
        copies[first + 2 * j].wait()
        copies[first + 2 * j + 1].wait()
        for n, out in enumerate(outs):
            at = slice(n * rows, (n + 1) * rows)
            acc = dot(g_held[0, at, 0:half], m_held[0, :, cols], (1, 0))
            acc += dot(g_held[0, at, half : 2 * half], m_held[1, :, cols], (1, 0))
            for k in range(3):
                acc += dot(g_held[k + 1, at, 0:half], x_held[0, j, k], (1, 0))
                acc += dot(g_held[k + 1, at, half : 2 * half], x_held[1, j, k], (1, 0))
            out[:, j * half : (j + 1) * half] = acc.astype(BF)


def product(place, start, count, rows, grads, mine, rest, own, other):
    tok = grads[0].shape[1]
    half, width = mine.shape
    return pl.pallas_call(
        functools.partial(product_kernel, start),
        out_shape=[jax.ShapeDtypeStruct((rows, width), BF)] * count,
        in_specs=scalars() + [pl.BlockSpec(memory_space=pl.ANY)] * 14,
        out_specs=vmem(count),
        scratch_shapes=[
            pltpu.VMEM((4, count * rows, tok), BF),
            pltpu.VMEM((2, half, width), BF),
            pltpu.VMEM((2, 4) + own[0].shape, BF),
            pltpu.SemaphoreType.DMA((14,)),
        ],
        compiler_params=pltpu.CompilerParams(vmem_limit_bytes=16 << 20),
        cost_estimate=pl.CostEstimate(
            flops=8 * count * rows * tok * width, bytes_accessed=6 << 20, transcendentals=0
        ),
    )(place, *grads, mine, rest, *own, *other)


def middle_kernel(place, m0, m1, m2, inverse, *refs):
    own, other, out, summed, scaled, held, sems = refs[0:4], refs[4:8], *refs[8:]
    z, h, c, x = place[0], place[1], place[2], place[3]
    quarter = m0.shape[0]
    copies = []
    for n, ref in enumerate(own + other):
        copies.append(pltpu.make_async_copy(ref, held.at[n // 4, n % 4], sems.at[n]))
        copies[-1].start()
    total = m0[...].astype(F32) + m1[...].astype(F32) + m2[...].astype(F32)
    summed[...] = total.astype(BF)
    for copy in copies:
        copy.wait()
    bases = [(core, side) for core in (0, 1) for side in (0, 1)]
    for n, (core, side) in enumerate(bases):
        acc = None
        for j in range(4):
            term = dot(summed[:, j * quarter : (j + 1) * quarter], held[core, j, side], (1, 0))
            acc = term if acc is None else acc + term
        q = 2 * jnp.bitwise_xor(h, side) + jnp.bitwise_xor(c, core)
        scaled[n] = (acc * inverse[jnp.bitwise_xor(z, q)].astype(F32)).astype(BF)
    for j in range(4):
        acc = None
        for n, (core, side) in enumerate(bases):
            term = dot(held[core, j, side], scaled[n], (1, 1))
            acc = term if acc is None else acc + term
        out[jnp.bitwise_xor(z, lax.rem(x + 4 - j, 4))] = acc.astype(BF)


def middle(place, sums, inverse, own, other):
    quarter, width = sums[0].shape
    return pl.pallas_call(
        middle_kernel,
        out_shape=jax.ShapeDtypeStruct((4, quarter, quarter), BF),
        in_specs=scalars() + vmem(4) + [pl.BlockSpec(memory_space=pl.ANY)] * 8,
        out_specs=pl.BlockSpec(memory_space=pltpu.VMEM),
        scratch_shapes=[
            pltpu.VMEM((quarter, width), BF),
            pltpu.VMEM((4, quarter, quarter), BF),
            pltpu.VMEM((2, 4) + own[0].shape, BF),
            pltpu.SemaphoreType.DMA((8,)),
        ],
        compiler_params=pltpu.CompilerParams(vmem_limit_bytes=16 << 20),
        cost_estimate=pl.CostEstimate(
            flops=4 * quarter * width * width, bytes_accessed=6 << 20, transcendentals=0
        ),
    )(place, *sums, inverse, *own, *other)


def last_kernel(place, basis, b0, b1, b2, b3, out):
    z = place[0]
    quarter = b0.shape[1]
    for n in range(0, out.shape[1], 512):
        acc = None
        for e, b in enumerate((b0, b1, b2, b3)):
            at = pl.multiple_of(jnp.bitwise_xor(z, e) * quarter, quarter)
            term = dot(b[...], basis[n : n + 512, pl.ds(at, quarter)], (1, 1))
            acc = term if acc is None else acc + term
        out[:, n : n + 512] = acc.astype(BF)


def last(place, basis, parts):
    rows = parts[0].shape[0]
    width = basis.shape[0]
    return pl.pallas_call(
        last_kernel,
        out_shape=jax.ShapeDtypeStruct((rows, width), BF),
        in_specs=scalars() + vmem(5),
        out_specs=pl.BlockSpec(memory_space=pltpu.VMEM),
        compiler_params=pltpu.CompilerParams(vmem_limit_bytes=14 << 20),
        cost_estimate=pl.CostEstimate(
            flops=2 * rows * width * width, bytes_accessed=3 << 20, transcendentals=0
        ),
    )(place, basis, *parts)


def on_device(inputs, out_grads, basis_in, basis_out, eigenvalues):
    tok = inputs.shape[0]
    block = basis_in.shape[0]
    quarter = block // 4
    half = tok // 2
    owner = lax.axis_index("owner")
    data = lax.axis_index("dp")
    x, h, c = owner // 4, owner // 2 % 2, owner % 2
    y, z = data // NZ, data % NZ
    place = jnp.stack([z, h, c, x]).astype(jnp.int32)

    def after(value, *earlier):
        return lax.optimization_barrier((value,) + earlier)[0]

    def piece(rows, b, col, width):
        return lax.dynamic_slice(inputs, (rows * half, b % NY * block + col), (half, width))

    got = {k: along_y(piece(c, y + k, x * quarter, quarter), k) for k in (1, 3, 2)}

    og = jnp.concatenate(
        [
            lax.dynamic_slice_in_dim(out_grads, c * half, half, 0),
            lax.dynamic_slice_in_dim(out_grads, (1 - c) * half, half, 0),
        ],
        0,
    )
    def turned(group):
        cols = [
            lax.dynamic_slice_in_dim(basis_out, (z ^ e) * quarter, quarter, 1) for e in group
        ]
        return dot(jnp.concatenate(cols, 1), og, (0, 1)).astype(BF)

    def spread(gt, *earlier):
        go = after(gt, *earlier)
        one = {k: along_y(go, k) for k in (1, 3, 2)}
        return [gt] + [one[k] for k in (1, 2, 3)]

    upper = spread(turned((3, 2)), got[1])
    lower = spread(turned((1, 0)), upper[1])

    def over_x(pieces):
        got = {j: along_x(pieces, j) for j in (1, 3)}
        got[2] = along_x(after(pieces, got[1]), 2)
        own = [pieces] + [got[j] for j in (1, 2, 3)]
        return own, [other_core(o) for o in own]

    own, other = over_x(jnp.stack([got[1], got[2], got[3]]))
    mine, rest = piece(c, y, 0, block), piece(1 - c, y, 0, block)

    inverse = (1.0 / (eigenvalues + DAMPING)).T.astype(BF)

    def level(e):
        return lax.dynamic_slice_in_dim(inverse, (z ^ e) * quarter, quarter, 0)

    inverse = jnp.stack([level(0)] + [across_z(after(level(e), own[1]), e) for e in (1, 2, 3)])

    local = (mine, rest, own, other)
    (m3,) = product(place, 0, 1, quarter, upper, *local)
    near3 = across_z(after(m3, inverse), 1)
    (m2,) = product(place, quarter, 1, quarter, upper, *local)
    far2 = (m2.astype(F32) + near3.astype(F32)).astype(BF)
    m1, m0 = product(place, 0, 2, quarter, lower, *local)
    near1 = across_z(m1, 1)

    at = lax.dynamic_slice_in_dim(after(basis_in, far2), y * quarter, quarter, 0)
    a_own, a_other = over_x(jnp.stack([crossed(at, 0), crossed(at, 1)]))
    parts = middle(place, [m0, near1, across_z(far2, 2)], inverse, a_own, a_other)
    parts = [parts[0]] + [across_z(parts[e], e) for e in (1, 2, 3)]
    return last(place, basis_out, parts)


def solution(mesh):
    placed = (P("dp", None), P("dp", "owner"), P(None, "owner"), P(None, "owner"), P("dp", "owner"))
    return jax.shard_map(
        on_device, mesh=mesh, in_specs=placed, out_specs=P("dp", "owner"), check_vma=False
    )
```

```python
import functools

import jax
import jax.numpy as jnp
from jax import lax
from jax.experimental import pallas as pl
from jax.experimental.pallas import tpu as pltpu
from jax.sharding import PartitionSpec as P

DAMPING = 0.05
COST = pl.CostEstimate(flops=1000, bytes_accessed=1000, transcendentals=0)
NX, NY, NZ = 4, 4, 4
BF = jnp.bfloat16
F32 = jnp.float32


def moved(block, place):
    route = []
    for y in range(NY):
        for z in range(NZ):
            for x in range(NX):
                for h in range(2):
                    for c in range(2):
                        tx, ty, tz, th, tc = place(x, y, z, h, c)
                        source = (y * NZ + z) * 16 + x * 4 + h * 2 + c
                        target = (ty % NY * NZ + tz % NZ) * 16 + tx % NX * 4 + th * 2 + tc
                        route.append((source, target))
    return lax.ppermute(block, ("dp", "owner"), route)


def along_x(block, k):
    return moved(block, lambda x, y, z, h, c: (x + k, y, z, h, c))


def along_y(block, k):
    return moved(block, lambda x, y, z, h, c: (x, y + k, z, h, c))


def across_z(block, e):
    return moved(block, lambda x, y, z, h, c: (x, y, z ^ e, h, c))


def crossed(block, flip):
    return moved(block, lambda x, y, z, h, c: (y, x, z, h ^ flip, c))


def other_core(block):
    return moved(block, lambda x, y, z, h, c: (x, y, z, h, 1 - c))


def dot(a, b, dims):
    return lax.dot_general(a, b, ((dims[:1], dims[1:]), ((), ())), preferred_element_type=F32)


def vmem(count):
    return [pl.BlockSpec(memory_space=pltpu.VMEM)] * count


def scalars():
    return [pl.BlockSpec(memory_space=pltpu.SMEM)]


def product_kernel(start, place, g0, g1, g2, g3, mine, rest, *refs):
    count = len(refs) - 12
    own, other, outs = refs[0:4], refs[4:8], refs[8 : 8 + count]
    g_held, m_held, x_held, sems = refs[8 + count :]
    x = place[3]
    half = mine.shape[0]
    rows = outs[0].shape[0]
    total = count * rows
    copies = []

    def fetch(source, target):
        copies.append(pltpu.make_async_copy(source, target, sems.at[len(copies)]))
        copies[-1].start()

    fetch(g0.at[pl.ds(start, total)], g_held.at[0])
    fetch(mine, m_held.at[0])
    fetch(rest, m_held.at[1])
    for k, g in enumerate((g1, g2, g3)):
        fetch(g.at[pl.ds(start, total)], g_held.at[k + 1])
    first = len(copies)
    for j in range(4):
        fetch(own[j], x_held.at[0, j])
        fetch(other[j], x_held.at[1, j])
    for copy in copies[:first]:
        copy.wait()
    for j in range(4):
        cols = pl.ds(pl.multiple_of(lax.rem(x + 4 - j, 4) * half, half), half)
        copies[first + 2 * j].wait()
        copies[first + 2 * j + 1].wait()
        for n, out in enumerate(outs):
            at = slice(n * rows, (n + 1) * rows)
            acc = dot(g_held[0, at, 0:half], m_held[0, :, cols], (1, 0))
            acc += dot(g_held[0, at, half : 2 * half], m_held[1, :, cols], (1, 0))
            for k in range(3):
                acc += dot(g_held[k + 1, at, 0:half], x_held[0, j, k], (1, 0))
                acc += dot(g_held[k + 1, at, half : 2 * half], x_held[1, j, k], (1, 0))
            out[:, j * half : (j + 1) * half] = acc.astype(BF)


def product(place, start, count, rows, grads, mine, rest, own, other):
    tok = grads[0].shape[1]
    half, width = mine.shape
    return pl.pallas_call(
        functools.partial(product_kernel, start),
        out_shape=[jax.ShapeDtypeStruct((rows, width), BF)] * count,
        in_specs=scalars() + [pl.BlockSpec(memory_space=pl.ANY)] * 14,
        out_specs=vmem(count),
        scratch_shapes=[
            pltpu.VMEM((4, count * rows, tok), BF),
            pltpu.VMEM((2, half, width), BF),
            pltpu.VMEM((2, 4) + own[0].shape, BF),
            pltpu.SemaphoreType.DMA((14,)),
        ],
        compiler_params=pltpu.CompilerParams(vmem_limit_bytes=48 << 20),
        cost_estimate=COST,
    )(place, *grads, mine, rest, *own, *other)


def middle_kernel(place, m0, m1, m2, inverse, *refs):
    own, other, out, summed, scaled, held, sems = refs[0:4], refs[4:8], *refs[8:]
    z, h, c, x = place[0], place[1], place[2], place[3]
    quarter = m0.shape[0]
    copies = []
    for n, ref in enumerate(own + other):
        copies.append(pltpu.make_async_copy(ref, held.at[n // 4, n % 4], sems.at[n]))
        copies[-1].start()
    total = m0[...].astype(F32) + m1[...].astype(F32) + m2[...].astype(F32)
    summed[...] = total.astype(BF)
    for copy in copies:
        copy.wait()
    bases = [(core, side) for core in (0, 1) for side in (0, 1)]
    for n, (core, side) in enumerate(bases):
        acc = None
        for j in range(4):
            term = dot(summed[:, j * quarter : (j + 1) * quarter], held[core, j, side], (1, 0))
            acc = term if acc is None else acc + term
        q = 2 * jnp.bitwise_xor(h, side) + jnp.bitwise_xor(c, core)
        scaled[n] = (acc * inverse[jnp.bitwise_xor(z, q)].astype(F32)).astype(BF)
    for j in range(4):
        acc = None
        for n, (core, side) in enumerate(bases):
            term = dot(held[core, j, side], scaled[n], (1, 1))
            acc = term if acc is None else acc + term
        out[jnp.bitwise_xor(z, lax.rem(x + 4 - j, 4))] = acc.astype(BF)


def middle(place, sums, inverse, own, other):
    quarter, width = sums[0].shape
    return pl.pallas_call(
        middle_kernel,
        out_shape=jax.ShapeDtypeStruct((4, quarter, quarter), BF),
        in_specs=scalars() + vmem(4) + [pl.BlockSpec(memory_space=pl.ANY)] * 8,
        out_specs=pl.BlockSpec(memory_space=pltpu.VMEM),
        scratch_shapes=[
            pltpu.VMEM((quarter, width), BF),
            pltpu.VMEM((4, quarter, quarter), BF),
            pltpu.VMEM((2, 4) + own[0].shape, BF),
            pltpu.SemaphoreType.DMA((8,)),
        ],
        compiler_params=pltpu.CompilerParams(vmem_limit_bytes=48 << 20),
        cost_estimate=COST,
    )(place, *sums, inverse, *own, *other)


def last_kernel(place, basis, b0, b1, b2, b3, out):
    z = place[0]
    quarter = b0.shape[1]
    for n in range(0, out.shape[1], 512):
        acc = None
        for e, b in enumerate((b0, b1, b2, b3)):
            at = pl.multiple_of(jnp.bitwise_xor(z, e) * quarter, quarter)
            term = dot(b[...], basis[n : n + 512, pl.ds(at, quarter)], (1, 1))
            acc = term if acc is None else acc + term
        out[:, n : n + 512] = acc.astype(BF)


def last(place, basis, parts):
    rows = parts[0].shape[0]
    width = basis.shape[0]
    return pl.pallas_call(
        last_kernel,
        out_shape=jax.ShapeDtypeStruct((rows, width), BF),
        in_specs=scalars() + vmem(5),
        out_specs=pl.BlockSpec(memory_space=pltpu.VMEM),
        compiler_params=pltpu.CompilerParams(vmem_limit_bytes=14 << 20),
        cost_estimate=COST,
    )(place, basis, *parts)


def on_device(inputs, out_grads, basis_in, basis_out, eigenvalues):
    tok = inputs.shape[0]
    block = basis_in.shape[0]
    quarter = block // 4
    half = tok // 2
    owner = lax.axis_index("owner")
    data = lax.axis_index("dp")
    x, h, c = owner // 4, owner // 2 % 2, owner % 2
    y, z = data // NZ, data % NZ
    place = jnp.stack([z, h, c, x]).astype(jnp.int32)

    def after(value, *earlier):
        return lax.optimization_barrier((value,) + earlier)[0]

    def piece(rows, b, col, width):
        return lax.dynamic_slice(inputs, (rows * half, b % NY * block + col), (half, width))

    to_send = {k: piece(c, y + k, x * quarter, quarter) for k in (1, 3, 2)}
    got = {k: along_y(to_send[k], k) for k in (1, 3, 2)}

    basis_in, out_grads = lax.optimization_barrier((basis_in, out_grads, to_send))[:2]
    at = lax.dynamic_slice_in_dim(basis_in, y * quarter, quarter, 0)
    pieces = jnp.stack([crossed(at, 0), crossed(at, 1)])

    og = jnp.concatenate(
        [
            lax.dynamic_slice_in_dim(out_grads, c * half, half, 0),
            lax.dynamic_slice_in_dim(out_grads, (1 - c) * half, half, 0),
        ],
        0,
    )
    def turned(group):
        cols = [
            lax.dynamic_slice_in_dim(basis_out, (z ^ e) * quarter, quarter, 1) for e in group
        ]
        return dot(jnp.concatenate(cols, 1), og, (0, 1)).astype(BF)

    def spread(gt, *earlier):
        go = after(gt, *earlier)
        one = {k: along_y(go, k) for k in (1, 3, 2)}
        return [gt] + [one[k] for k in (1, 2, 3)]

    upper = spread(turned((3, 2)), pieces)
    lower = spread(turned((1, 0)), upper[1], pieces)

    def over_x(pieces):
        got = {j: along_x(pieces, j) for j in (1, 3)}
        got[2] = along_x(after(pieces, got[1]), 2)
        own = [pieces] + [got[j] for j in (1, 2, 3)]
        return own, [other_core(o) for o in own]

    own, other = over_x(jnp.stack([got[1], got[2], got[3]]))
    mine, rest = piece(c, y, 0, block), piece(1 - c, y, 0, block)

    inverse = (1.0 / (eigenvalues + DAMPING)).T.astype(BF)

    def level(e):
        return lax.dynamic_slice_in_dim(inverse, (z ^ e) * quarter, quarter, 0)

    inverse = jnp.stack([level(0)] + [across_z(after(level(e), upper[1], pieces), e) for e in (1, 2, 3)])

    local = (mine, rest, own, other)
    (m3,) = product(place, 0, 1, quarter, upper, *local)
    near3 = across_z(after(m3, inverse), 1)
    (m2,) = product(place, quarter, 1, quarter, upper, *local)
    far2 = (m2.astype(F32) + near3.astype(F32)).astype(BF)
    lower[0] = after(lower[0], far2)
    m1, m0 = product(place, 0, 2, quarter, lower, *local)
    near1 = across_z(m1, 1)

    a_own, a_other = over_x(after(pieces, far2))
    parts = middle(place, [m0, near1, across_z(far2, 2)], inverse, a_own, a_other)
    parts = [parts[0]] + [across_z(parts[e], e) for e in (1, 2, 3)]
    return last(place, basis_out, parts)


def solution(mesh):
    placed = (P("dp", None), P("dp", "owner"), P(None, "owner"), P(None, "owner"), P("dp", "owner"))
    return jax.shard_map(
        on_device, mesh=mesh, in_specs=placed, out_specs=P("dp", "owner"), check_vma=False
    )
```

```python
import functools

import jax
import jax.numpy as jnp
from jax import lax
from jax.experimental import pallas as pl
from jax.experimental.pallas import tpu as pltpu
from jax.sharding import PartitionSpec as P

DAMPING = 0.05
COST = pl.CostEstimate(flops=1000, bytes_accessed=1000, transcendentals=0)
NX, NY, NZ = 4, 4, 4
BF = jnp.bfloat16
F32 = jnp.float32


def moved(block, place):
    route = []
    for y in range(NY):
        for z in range(NZ):
            for x in range(NX):
                for h in range(2):
                    for c in range(2):
                        tx, ty, tz, th, tc = place(x, y, z, h, c)
                        source = (y * NZ + z) * 16 + x * 4 + h * 2 + c
                        target = (ty % NY * NZ + tz % NZ) * 16 + tx % NX * 4 + th * 2 + tc
                        route.append((source, target))
    return lax.ppermute(block, ("dp", "owner"), route)


def along_x(block, k):
    return moved(block, lambda x, y, z, h, c: (x + k, y, z, h, c))


def along_y(block, k):
    return moved(block, lambda x, y, z, h, c: (x, y + k, z, h, c))


def across_z(block, e):
    return moved(block, lambda x, y, z, h, c: (x, y, z ^ e, h, c))


def crossed(block, flip):
    return moved(block, lambda x, y, z, h, c: (y, x, z, h ^ flip, c))


def other_core(block):
    return moved(block, lambda x, y, z, h, c: (x, y, z, h, 1 - c))


def dot(a, b, dims):
    return lax.dot_general(a, b, ((dims[:1], dims[1:]), ((), ())), preferred_element_type=F32)


def vmem(count):
    return [pl.BlockSpec(memory_space=pltpu.VMEM)] * count


def scalars():
    return [pl.BlockSpec(memory_space=pltpu.SMEM)]


def product_kernel(start, place, g0, g1, g2, g3, mine, rest, *refs):
    count = len(refs) - 12
    own, other, outs = refs[0:4], refs[4:8], refs[8 : 8 + count]
    g_held, m_held, x_held, sems = refs[8 + count :]
    x = place[3]
    half = mine.shape[0]
    rows = outs[0].shape[0]
    total = count * rows
    copies = []

    def fetch(source, target):
        copies.append(pltpu.make_async_copy(source, target, sems.at[len(copies)]))
        copies[-1].start()

    fetch(g0.at[pl.ds(start, total)], g_held.at[0])
    fetch(mine, m_held.at[0])
    fetch(rest, m_held.at[1])
    for k, g in enumerate((g1, g2, g3)):
        fetch(g.at[pl.ds(start, total)], g_held.at[k + 1])
    first = len(copies)
    for j in range(4):
        fetch(own[j], x_held.at[0, j])
        fetch(other[j], x_held.at[1, j])
    for copy in copies[:first]:
        copy.wait()
    for j in range(4):
        cols = pl.ds(pl.multiple_of(lax.rem(x + 4 - j, 4) * half, half), half)
        copies[first + 2 * j].wait()
        copies[first + 2 * j + 1].wait()
        for n, out in enumerate(outs):
            at = slice(n * rows, (n + 1) * rows)
            acc = dot(g_held[0, at, 0:half], m_held[0, :, cols], (1, 0))
            acc += dot(g_held[0, at, half : 2 * half], m_held[1, :, cols], (1, 0))
            for k in range(3):
                acc += dot(g_held[k + 1, at, 0:half], x_held[0, j, k], (1, 0))
                acc += dot(g_held[k + 1, at, half : 2 * half], x_held[1, j, k], (1, 0))
            out[:, j * half : (j + 1) * half] = acc.astype(BF)


def product(place, start, count, rows, grads, mine, rest, own, other):
    tok = grads[0].shape[1]
    half, width = mine.shape
    return pl.pallas_call(
        functools.partial(product_kernel, start),
        out_shape=[jax.ShapeDtypeStruct((rows, width), BF)] * count,
        in_specs=scalars() + [pl.BlockSpec(memory_space=pl.ANY)] * 14,
        out_specs=vmem(count),
        scratch_shapes=[
            pltpu.VMEM((4, count * rows, tok), BF),
            pltpu.VMEM((2, half, width), BF),
            pltpu.VMEM((2, 4) + own[0].shape, BF),
            pltpu.SemaphoreType.DMA((14,)),
        ],
        compiler_params=pltpu.CompilerParams(vmem_limit_bytes=48 << 20),
        cost_estimate=COST,
    )(place, *grads, mine, rest, *own, *other)


def middle_kernel(place, m0, m1, m2, inverse, *refs):
    own, other, out, summed, scaled, held, sems = refs[0:4], refs[4:8], *refs[8:]
    z, h, c, x = place[0], place[1], place[2], place[3]
    quarter = m0.shape[0]
    copies = []
    for n, ref in enumerate(own + other):
        copies.append(pltpu.make_async_copy(ref, held.at[n // 4, n % 4], sems.at[n]))
        copies[-1].start()
    total = m0[...].astype(F32) + m1[...].astype(F32) + m2[...].astype(F32)
    summed[...] = total.astype(BF)
    for copy in copies:
        copy.wait()
    bases = [(core, side) for core in (0, 1) for side in (0, 1)]
    for n, (core, side) in enumerate(bases):
        acc = None
        for j in range(4):
            term = dot(summed[:, j * quarter : (j + 1) * quarter], held[core, j, side], (1, 0))
            acc = term if acc is None else acc + term
        q = 2 * jnp.bitwise_xor(h, side) + jnp.bitwise_xor(c, core)
        scaled[n] = (acc * inverse[jnp.bitwise_xor(z, q)].astype(F32)).astype(BF)
    for j in range(4):
        acc = None
        for n, (core, side) in enumerate(bases):
            term = dot(held[core, j, side], scaled[n], (1, 1))
            acc = term if acc is None else acc + term
        out[jnp.bitwise_xor(z, lax.rem(x + 4 - j, 4))] = acc.astype(BF)


def middle(place, sums, inverse, own, other):
    quarter, width = sums[0].shape
    return pl.pallas_call(
        middle_kernel,
        out_shape=jax.ShapeDtypeStruct((4, quarter, quarter), BF),
        in_specs=scalars() + vmem(4) + [pl.BlockSpec(memory_space=pl.ANY)] * 8,
        out_specs=pl.BlockSpec(memory_space=pltpu.VMEM),
        scratch_shapes=[
            pltpu.VMEM((quarter, width), BF),
            pltpu.VMEM((4, quarter, quarter), BF),
            pltpu.VMEM((2, 4) + own[0].shape, BF),
            pltpu.SemaphoreType.DMA((8,)),
        ],
        compiler_params=pltpu.CompilerParams(vmem_limit_bytes=48 << 20),
        cost_estimate=COST,
    )(place, *sums, inverse, *own, *other)


def last_kernel(place, basis, b0, b1, b2, b3, out):
    z = place[0]
    quarter = b0.shape[1]
    for n in range(0, out.shape[1], 512):
        acc = None
        for e, b in enumerate((b0, b1, b2, b3)):
            at = pl.multiple_of(jnp.bitwise_xor(z, e) * quarter, quarter)
            term = dot(b[...], basis[n : n + 512, pl.ds(at, quarter)], (1, 1))
            acc = term if acc is None else acc + term
        out[:, n : n + 512] = acc.astype(BF)


def last(place, basis, parts):
    rows = parts[0].shape[0]
    width = basis.shape[0]
    return pl.pallas_call(
        last_kernel,
        out_shape=jax.ShapeDtypeStruct((rows, width), BF),
        in_specs=scalars() + vmem(5),
        out_specs=pl.BlockSpec(memory_space=pltpu.VMEM),
        compiler_params=pltpu.CompilerParams(vmem_limit_bytes=14 << 20),
        cost_estimate=COST,
    )(place, basis, *parts)


def on_device(inputs, out_grads, basis_in, basis_out, eigenvalues):
    tok = inputs.shape[0]
    block = basis_in.shape[0]
    quarter = block // 4
    half = tok // 2
    owner = lax.axis_index("owner")
    data = lax.axis_index("dp")
    x, h, c = owner // 4, owner // 2 % 2, owner % 2
    y, z = data // NZ, data % NZ
    place = jnp.stack([z, h, c, x]).astype(jnp.int32)

    def after(value, *earlier):
        return lax.optimization_barrier((value,) + earlier)[0]

    def piece(rows, b, col, width):
        return lax.dynamic_slice(inputs, (rows * half, b % NY * block + col), (half, width))

    to_send = {k: piece(c, y + k, x * quarter, quarter) for k in (1, 3, 2)}
    got = {k: along_y(to_send[k], k) for k in (1, 3, 2)}

    basis_in, out_grads = lax.optimization_barrier((basis_in, out_grads, to_send))[:2]
    at = lax.dynamic_slice_in_dim(basis_in, y * quarter, quarter, 0)
    pieces = jnp.stack([crossed(at, 0), crossed(at, 1)])

    og = jnp.concatenate(
        [
            lax.dynamic_slice_in_dim(out_grads, c * half, half, 0),
            lax.dynamic_slice_in_dim(out_grads, (1 - c) * half, half, 0),
        ],
        0,
    )
    def turned(group):
        cols = [
            lax.dynamic_slice_in_dim(basis_out, (z ^ e) * quarter, quarter, 1) for e in group
        ]
        return dot(jnp.concatenate(cols, 1), og, (0, 1)).astype(BF)

    def spread(gt, *earlier):
        go = after(gt, *earlier)
        one = {k: along_y(go, k) for k in (1, 3, 2)}
        return [gt] + [one[k] for k in (1, 2, 3)]

    upper = spread(turned((3, 2)), pieces)
    lower = spread(turned((1, 0)), upper[1], pieces)

    def over_x(pieces):
        got = {j: along_x(pieces, j) for j in (1, 3)}
        got[2] = along_x(after(pieces, got[1]), 2)
        own = [pieces] + [got[j] for j in (1, 2, 3)]
        return own, [other_core(o) for o in own]

    own, other = over_x(jnp.stack([got[1], got[2], got[3]]))
    mine, rest = piece(c, y, 0, block), piece(1 - c, y, 0, block)

    inverse = (1.0 / (eigenvalues + DAMPING)).T.astype(BF)

    def level(e):
        return lax.dynamic_slice_in_dim(inverse, (z ^ e) * quarter, quarter, 0)

    inverse = jnp.stack([level(0)] + [across_z(after(level(e), upper[1], pieces, own[2]), e) for e in (1, 2, 3)])

    local = (mine, rest, own, other)
    (m3,) = product(place, 0, 1, quarter, upper, *local)
    near3 = across_z(after(m3, inverse), 1)
    (m2,) = product(place, quarter, 1, quarter, upper, *local)
    far2 = (m2.astype(F32) + near3.astype(F32)).astype(BF)
    lower[0] = after(lower[0], far2)
    m1, m0 = product(place, 0, 2, quarter, lower, *local)
    near1 = across_z(m1, 1)

    a_own, a_other = over_x(after(pieces, far2))
    parts = middle(place, [m0, near1, across_z(far2, 2)], inverse, a_own, a_other)
    parts = [parts[0]] + [across_z(parts[e], e) for e in (1, 2, 3)]
    return last(place, basis_out, parts)


def solution(mesh):
    placed = (P("dp", None), P("dp", "owner"), P(None, "owner"), P(None, "owner"), P("dp", "owner"))
    return jax.shard_map(
        on_device, mesh=mesh, in_specs=placed, out_specs=P("dp", "owner"), check_vma=False
    )
```
